32 devices in a mesh: dp: 8 (over z, x), seq: 4 (over y, core).
Axes of the slice: x: 2, y: 2, z: 4, core: 2. Of those that a mesh axis runs over, the one named last changes fastest.
Arguments:
- tokens: bfloat16 [8, 1024, 768], P('dp', 'seq'), may hold values from -6 to 6
- norm_gain: float32 [768], P('dp'), may hold values from 0.5 to 1.5
- in_weight: bfloat16 [768, 3352], P('dp'), may hold values from -0.21875 to 0.21875
- conv_weight: float32 [4, 1792], P(None, 'dp'), may hold values from -3 to 3
- conv_bias: float32 [1792], P('dp'), may hold values from -0.5 to 0.5
- dt_bias: float32 [24], replicated, may hold values from -4.5 to -3
- a_log: float32 [24], replicated, as said below
- skip: float32 [24], replicated, may hold values from 0.5 to 1.5
- gate_norm: float32 [1536], P('dp'), may hold values from 0.5 to 1.5
- out_weight: bfloat16 [1536, 768], P('dp'), may hold values from -0.15625 to 0.15625
- cotangent: bfloat16 [8, 1024, 768], P('dp', 'seq'), may hold values from -6 to 6
Outputs:
- mixed: bfloat16 [8, 1024, 768], P('dp', 'seq')
- grad_tokens: bfloat16 [8, 1024, 768], P('dp', 'seq')
- grad_norm_gain: float32 [768], P('dp')
- grad_in_weight: float32 [768, 3352], P('dp')
- grad_conv_weight: float32 [4, 1792], P(None, 'dp')
- grad_conv_bias: float32 [1792], P('dp')
- grad_dt_bias: float32 [24], replicated
- grad_a_log: float32 [24], replicated
- grad_skip: float32 [24], replicated
- grad_gate_norm: float32 [1536], P('dp')
- grad_out_weight: float32 [1536, 768], P('dp')
The draws below stay inside these ranges and needn't reach their ends.
Inputs may be any that keep to these rules, and one draw needn't show every extreme that they name: exp(a_log) lies between 4 / 1024 and 0.6.
All inputs are finite; a program needn't handle non-finite values.
Results may differ from the reference program's by a relative error of at most 0.018.
Values may be sent and summed in bfloat16 or wider, within the bound.
A program may use at most 128 MiB of HBM per device.

```python
import jax
import jax.numpy as jnp
from jax import lax

D = 768
HEADS = 24
HEAD = 64
STATE = 128
KCONV = 4
PIECE = 256
INNER = 1536
CONV_CH = 1792
IN_W = 3352
LENGTH = 1024
BATCH = 8


def draw_a_log(key, part):
    key = jax.random.fold_in(key, 7)
    spread = jax.random.uniform(key, (HEADS,), jnp.float32)
    slow_end = jnp.log(4.0 / LENGTH)
    fast_end = jnp.log(0.6)
    return slow_end + (fast_end - slow_end) * spread


def block_levels(stream_key, shape, cuts, low, high):
    def one(axis_at, shards_of):
        draws = jax.random.uniform(jax.random.fold_in(jax.random.fold_in(stream_key, 6), axis_at), (shards_of,), jnp.float32, low / len(cuts), high / len(cuts))
        return jnp.repeat(jnp.exp(draws), shape[axis_at] // shards_of).reshape((-1,) + (1,) * (len(shape) - axis_at - 1))

    gain = one(*cuts[0])
    for cut in cuts[1:]:
        gain = gain * one(*cut)
    return gain


def noise(key, extent, deviation, most, shards=(), dtype=jnp.bfloat16):
    factor_of = block_levels(key, extent, shards, -0.22, 0.18) if shards else 1.0
    values = jax.random.normal(key, extent, jnp.float32) * deviation * factor_of
    return jnp.minimum(jnp.maximum(values, -most), most).astype(dtype)


def setup_inputs(seed: int = 0) -> dict:
    streams_of = jax.random.split(jax.random.key(seed), 12)
    tokens = noise(streams_of[0], (BATCH, LENGTH, D), 1.0, 6.0, ((0, 8), (1, 4)))
    norm_gain = jnp.clip(1.0 + 0.1 * jax.random.normal(streams_of[1], (D,), jnp.float32), 0.5, 1.5)
    in_weight = noise(streams_of[2], (D, IN_W), D ** -0.5, 0.21875, ((0, 8),))
    conv_weight = noise(streams_of[3], (KCONV, CONV_CH), KCONV ** -0.5, 3.0, ((1, 8),), jnp.float32)
    conv_bias = jnp.clip(jax.random.uniform(streams_of[4], (CONV_CH,), jnp.float32, -0.5, 0.5) * block_levels(streams_of[4], (CONV_CH,), ((0, 8),), -0.4, 0.0), -0.5, 0.5)
    dt_bias = jnp.clip(jax.random.uniform(streams_of[5], (HEADS,), jnp.float32, -4.5, -3.0), -4.5, -3.0)
    a_log = draw_a_log(jax.random.fold_in(streams_of[11], 71), 0)
    skip = jnp.clip(jax.random.uniform(streams_of[7], (HEADS,), jnp.float32, 0.5, 1.5), 0.5, 1.5)
    gate_norm = jnp.clip(1.0 + 0.1 * jax.random.normal(streams_of[8], (INNER,), jnp.float32), 0.5, 1.5)
    out_weight = noise(streams_of[9], (INNER, D), INNER ** -0.5, 0.15625, ((0, 8),))
    cotangent = noise(streams_of[10], (BATCH, LENGTH, D), 1.0, 6.0, ((0, 8), (1, 4)))
    return dict(tokens=tokens, norm_gain=norm_gain, in_weight=in_weight, conv_weight=conv_weight, conv_bias=conv_bias, dt_bias=dt_bias, a_log=a_log, skip=skip, gate_norm=gate_norm, out_weight=out_weight, cotangent=cotangent)


EPS = 1e-05
HIGH = lax.Precision.HIGHEST

@jax.custom_vjp
def low(v):
    return lax.optimization_barrier(v.astype(jnp.bfloat16)).astype(jnp.float32)

@jax.custom_vjp
def low_back(v):
    return v

def low_keep(v):
    return (low(v), None)

def low_pass(kept, grad):
    return (grad,)

def back_keep(v):
    return (v, None)

def back_low(kept, grad):
    return (low(grad),)
low.defvjp(low_keep, low_pass)
low_back.defvjp(back_keep, back_low)

def matmul(left, right):
    return jnp.dot(left, right, precision=HIGH)

def block_step(s_in, block):
    xs, bm, cm, dtv, dav = block
    cum = jnp.cumsum(dav, 0).T
    count = cum.shape[1]
    lower = jnp.arange(count)[:, None] >= jnp.arange(count)[None, :]
    seg = jnp.where(lower[None], cum[:, :, None] - cum[:, None, :], -1e+30)
    lmat = jnp.exp(seg)
    gram = low_back(matmul(cm, bm.T))
    wmat = low(gram[None] * lmat * dtv.T[:, None, :])
    y_diag = jnp.einsum('htu,uhp->thp', wmat, xs, precision=HIGH)
    endc = cum[:, -1]
    bw = low(bm[None] * (jnp.exp(endc[:, None] - cum) * dtv.T)[:, :, None])
    s_loc = low_back(jnp.einsum('hun,uhp->hpn', bw, xs, precision=HIGH))
    ce = low(cm[None] * jnp.exp(cum)[:, :, None])
    y_off = jnp.einsum('htn,hpn->thp', ce, low(s_in), precision=HIGH)
    s_out = jnp.exp(endc)[:, None, None] * s_in + s_loc
    return (s_out, y_diag + y_off)

def forward(x_in, norm_gain, in_weight, conv_weight, conv_bias, dt_bias, a_log, skip, gate_norm, out_weight):
    rinv = lax.rsqrt(lax.optimization_barrier(jnp.mean(x_in * x_in, -1, keepdims=True)) + EPS)
    hval = low(x_in * rinv * norm_gain)
    proj = low_back(matmul(hval, in_weight))
    zval = proj[:, :INNER]
    xbc = low(proj[:, INNER:INNER + CONV_CH])
    dt_raw = proj[:, INNER + CONV_CH:]
    padded = jnp.concatenate([jnp.zeros((KCONV - 1, CONV_CH), jnp.float32), xbc], 0)
    pre = conv_bias + conv_weight[0] * padded[0:LENGTH]
    for k in range(1, KCONV):
        pre = pre + conv_weight[k] * padded[k:k + LENGTH]
    xconv = jax.nn.silu(pre)
    xs = low(xconv[:, :INNER])
    bm = low(xconv[:, INNER:INNER + STATE])
    cm = low(xconv[:, INNER + STATE:])
    dtv = jax.nn.softplus(dt_raw + dt_bias)
    dav = dtv * -jnp.exp(a_log)
    blocks = LENGTH // PIECE
    pieces = (xs.reshape(blocks, PIECE, HEADS, HEAD), bm.reshape(blocks, PIECE, STATE), cm.reshape(blocks, PIECE, STATE), dtv.reshape(blocks, PIECE, HEADS), dav.reshape(blocks, PIECE, HEADS))
    start = jnp.zeros((HEADS, HEAD, STATE), jnp.float32)
    _, ys = lax.scan(jax.checkpoint(block_step), start, pieces)
    yval = low_back(ys.reshape(LENGTH, INNER) + xs * jnp.repeat(skip, HEAD))
    gated = yval * jax.nn.silu(zval)
    grinv = lax.rsqrt(lax.optimization_barrier(jnp.mean(gated * gated, -1, keepdims=True)) + EPS)
    normed = low(gated * grinv * gate_norm)
    return x_in + matmul(normed, out_weight)

def reference(tokens, norm_gain, in_weight, conv_weight, conv_bias, dt_bias, a_log, skip, gate_norm, out_weight, cotangent):
    params = (norm_gain, in_weight.astype(jnp.float32), conv_weight, conv_bias, dt_bias, a_log, skip, gate_norm, out_weight.astype(jnp.float32))

    def one(total, pair):
        seq_in, seq_cot = pair
        result, pull = jax.vjp(forward, seq_in.astype(jnp.float32), *params)
        grads = pull(seq_cot.astype(jnp.float32))
        total = tuple((a + b for a, b in zip(total, grads[1:])))
        return (total, (result.astype(jnp.bfloat16), grads[0].astype(jnp.bfloat16)))
    zeros = tuple((jnp.zeros_like(p) for p in params))
    total, (mixed, grad_tokens) = lax.scan(one, zeros, (tokens, cotangent))
    return (mixed, grad_tokens, total[0], total[1], total[2], total[3], total[4], total[5], total[6], total[7], total[8])
```

```python
import functools

import jax
import jax.numpy as jnp
from jax import lax
from jax.experimental import pallas as pl
from jax.experimental.pallas import tpu as pltpu
from jax.sharding import PartitionSpec as P

HEADS = 24
HEAD = 64
STATE = 128
KCONV = 4
EPS = 1e-05
MESH = pl.DeviceIdType.MESH
F32 = jnp.float32
B16 = jnp.bfloat16


def ring_place(device, n):
    odd = device % 2
    return (1 - odd) * (device // 2) + odd * (n - 1 - device // 2)


def ring_device(place, n):
    place = (place + n) % n
    late = (2 * place) // n
    return (1 - late) * (2 * place) + late * (2 * (n - 1 - place) + 1)


def remote(src, dst, send, recv, target):
    return pltpu.make_async_remote_copy(
        src_ref=src, dst_ref=dst, send_sem=send, recv_sem=recv, device_id=target, device_id_type=MESH
    )


def greet(targets):
    barrier = pltpu.get_barrier_semaphore()
    for target in targets:
        pl.semaphore_signal(barrier, inc=1, device_id=target, device_id_type=MESH)
    pl.semaphore_wait(barrier, len(targets))


def gather_kernel(
    n, win, wout, small, gin, gout, gsmall, ring_send, ring_recv, core_send, core_recv
):
    d = lax.axis_index("dp")
    s = lax.axis_index("seq")
    c = s % 2
    p = ring_place(d, n)
    ahead = (ring_device(p + 1, n), s)
    behind = (ring_device(p - 1, n), s)
    other = (d, s + 1 - 2 * c)
    greet([ahead, behind, other])
    up = n // 2
    down = n - 1 - up
    pending = []

    def hop(index, origin, target, first):
        sources = (
            (win.at[c], wout.at[c], small)
            if first
            else (gin.at[c, origin], gout.at[c, origin], gsmall.at[origin])
        )
        dests = (gin.at[c, origin], gout.at[c, origin], gsmall.at[origin])
        copies = [
            remote(src, dst, ring_send.at[j, index], ring_recv.at[j, index], target)
            for j, (src, dst) in enumerate(zip(sources, dests))
        ]
        for copy in copies:
            copy.start()
        return copies

    def share(index, origin):
        for j, ref in enumerate((gin, gout)):
            copy = remote(
                ref.at[c, origin],
                ref.at[c, origin],
                core_send.at[j, index],
                core_recv.at[j, index],
                other,
            )
            copy.start()
            pending.append(copy)

    cw = hop(0, d, ahead, True)
    ccw = hop(up, d, behind, True)
    gin[0, d] = win[0]
    gin[1, d] = win[1]
    gout[0, d] = wout[0]
    gout[1, d] = wout[1]
    gsmall[d] = small[...]
    sent = list(cw) + list(ccw)
    for k in range(up):
        for copy in cw:
            copy.wait_recv()
        origin = ring_device(p - 1 - k, n)
        if k + 1 < up:
            cw = hop(k + 1, origin, ahead, False)
            sent += cw
        share(k, origin)
        if k < down:
            for copy in ccw:
                copy.wait_recv()
            origin = ring_device(p + 1 + k, n)
            if k + 1 < down:
                ccw = hop(up + k + 1, origin, behind, False)
                sent += ccw
            share(up + k, origin)
    for copy in sent:
        copy.wait_send()
    for copy in pending:
        copy.wait_send()
        copy.wait_recv()


def gather_all(win, wout, small, n):
    _, rows, cols = win.shape
    _, orows, ocols = wout.shape
    srows = small.shape[0]
    vmem = pl.BlockSpec(memory_space=pltpu.VMEM)
    return pl.pallas_call(
        functools.partial(gather_kernel, n),
        out_shape=(
            jax.ShapeDtypeStruct((2, n, rows, cols), B16),
            jax.ShapeDtypeStruct((2, n, orows, ocols), B16),
            jax.ShapeDtypeStruct((n, srows, 128), F32),
        ),
        in_specs=[vmem] * 3,
        out_specs=(vmem,) * 3,
        scratch_shapes=[
            pltpu.SemaphoreType.DMA((3, n - 1)),
            pltpu.SemaphoreType.DMA((3, n - 1)),
            pltpu.SemaphoreType.DMA((2, n - 1)),
            pltpu.SemaphoreType.DMA((2, n - 1)),
        ],
        compiler_params=pltpu.CompilerParams(
            collective_id=0, has_side_effects=True, vmem_limit_bytes=40 * 2**20
        ),
        name="gather_weights",
    )(win, wout, small)


def reduce_kernel(
    n,
    ny,
    pin,
    pout,
    psmall,
    phead,
    oin,
    oout,
    osmall,
    ohead,
    cin,
    cout,
    csmall,
    chead,
    sin,
    sout,
    ssmall,
    rin,
    rout,
    rsmall,
    hall,
    yin,
    yout,
    ysmall,
    yhead,
    fin,
    fout,
    core_send,
    core_recv,
    small_send,
    small_recv,
    ring_send,
    ring_recv,
    y_send,
    y_recv,
    end_send,
    end_recv,
):
    d = lax.axis_index("dp")
    s = lax.axis_index("seq")
    c = s % 2
    y = s // 2
    p = ring_place(d, n)
    ahead = (ring_device(p + 1, n), s)
    behind = (ring_device(p - 1, n), s)
    other = (d, s + 1 - 2 * c)
    peers = [(d, ((y + j) % ny) * 2 + c) for j in range(1, ny)]
    greet([ahead, behind, other] + peers)
    up = n // 2
    down = n - 1 - up
    sent = []

    small_copies = [
        remote(psmall, csmall, small_send.at[0], small_recv.at[0], other),
        remote(phead, chead, small_send.at[1], small_recv.at[1], other),
    ]
    for copy in small_copies:
        copy.start()
    order = []
    for k in range(up):
        order.append(up - k)
        if k < down:
            order.append(k - down)
    order.append(0)
    swaps = {}
    for j, offset in enumerate(order):
        t = ring_device(p + offset, n)
        swaps[offset] = [
            remote(pin.at[1 - c, t], cin.at[t], core_send.at[0, j], core_recv.at[0, j], other),
            remote(pout.at[1 - c, t], cout.at[t], core_send.at[1, j], core_recv.at[1, j], other),
        ]
        for copy in swaps[offset]:
            copy.start()
    for copy in small_copies:
        copy.wait()
    hall[d] = phead[...] + chead[...]

    def partial(offset):
        for copy in swaps[offset]:
            copy.wait_recv()
        t = ring_device(p + offset, n)
        return (
            t,
            pin[c, t].astype(F32) + cin[t].astype(F32),
            pout[c, t].astype(F32) + cout[t].astype(F32),
            psmall[t] + csmall[t],
        )

    def hop(slot, offset, before, origin, target):
        t, a, b, e = partial(offset)
        if before is not None:
            a = a + rin[before].astype(F32)
            b = b + rout[before].astype(F32)
            e = e + rsmall[before]
        sin[t] = a.astype(B16)
        sout[t] = b.astype(B16)
        ssmall[t] = e
        pairs = (
            (sin.at[t], rin.at[slot]),
            (sout.at[t], rout.at[slot]),
            (ssmall.at[t], rsmall.at[slot]),
            (hall.at[origin], hall.at[origin]),
        )
        copies = [
            remote(src, dst, ring_send.at[j, slot], ring_recv.at[j, slot], target)
            for j, (src, dst) in enumerate(pairs)
        ]
        for copy in copies:
            copy.start()
        sent.extend(copies)
        return copies

    cw = None
    ccw = None
    for k in range(up):
        if cw is not None:
            for copy in cw:
                copy.wait_recv()
        cw = hop(k, up - k, k - 1 if k else None, ring_device(p - k, n), ahead)
        if k < down:
            if ccw is not None:
                for copy in ccw:
                    copy.wait_recv()
            slot = up + k
            ccw = hop(slot, k - down, slot - 1 if k else None, ring_device(p + k, n), behind)
    _, a, b, e = partial(0)
    for copy in ccw:
        copy.wait_recv()
    last = up + down - 1
    a = a + rin[last].astype(F32)
    b = b + rout[last].astype(F32)
    e = e + rsmall[last]
    for copy in cw:
        copy.wait_recv()
    a = a + rin[up - 1].astype(F32)
    b = b + rout[up - 1].astype(F32)
    e = e + rsmall[up - 1]
    head = hall[0]
    for j in range(1, n):
        head = head + hall[j]
    yin[y] = a.astype(B16)
    yout[y] = b.astype(B16)
    ysmall[y] = e
    yhead[y] = head
    across = []
    for i, peer in enumerate(peers):
        for j, ref in enumerate((yin, yout, ysmall, yhead)):
            copy = remote(ref.at[y], ref.at[y], y_send.at[j, i], y_recv.at[j, i], peer)
            copy.start()
            across.append(copy)
    for copy in across:
        copy.wait_recv()
    a = yin[0].astype(F32)
    b = yout[0].astype(F32)
    e = ysmall[0]
    head = yhead[0]
    for j in range(1, ny):
        a = a + yin[j].astype(F32)
        b = b + yout[j].astype(F32)
        e = e + ysmall[j]
        head = head + yhead[j]
    fin[c] = a.astype(B16)
    fout[c] = b.astype(B16)
    ends = [
        remote(fin.at[c], fin.at[c], end_send.at[0], end_recv.at[0], other),
        remote(fout.at[c], fout.at[c], end_send.at[1], end_recv.at[1], other),
    ]
    for copy in ends:
        copy.start()
    osmall[...] = e
    ohead[...] = head
    for offset in order:
        for copy in swaps[offset]:
            copy.wait_send()
    for copy in sent:
        copy.wait_send()
    for copy in across:
        copy.wait_send()
    for copy in ends:
        copy.wait()
    oin[...] = fin[...].astype(F32)
    oout[...] = fout[...].astype(F32)


def reduce_all(pin, pout, psmall, phead, n, ny):
    _, _, rows, cols = pin.shape
    _, _, orows, ocols = pout.shape
    srows = psmall.shape[1]
    vmem = pl.BlockSpec(memory_space=pltpu.VMEM)
    many = max(ny - 1, 1)
    return pl.pallas_call(
        functools.partial(reduce_kernel, n, ny),
        out_shape=(
            jax.ShapeDtypeStruct((2, rows, cols), F32),
            jax.ShapeDtypeStruct((2, orows, ocols), F32),
            jax.ShapeDtypeStruct((srows, 128), F32),
            jax.ShapeDtypeStruct((8, 128), F32),
        ),
        in_specs=[vmem] * 4,
        out_specs=(vmem,) * 4,
        scratch_shapes=[
            pltpu.VMEM((n, rows, cols), B16),
            pltpu.VMEM((n, orows, ocols), B16),
            pltpu.VMEM((n, srows, 128), F32),
            pltpu.VMEM((8, 128), F32),
            pltpu.VMEM((n, rows, cols), B16),
            pltpu.VMEM((n, orows, ocols), B16),
            pltpu.VMEM((n, srows, 128), F32),
            pltpu.VMEM((n - 1, rows, cols), B16),
            pltpu.VMEM((n - 1, orows, ocols), B16),
            pltpu.VMEM((n - 1, srows, 128), F32),
            pltpu.VMEM((n, 8, 128), F32),
            pltpu.VMEM((ny, rows, cols), B16),
            pltpu.VMEM((ny, orows, ocols), B16),
            pltpu.VMEM((ny, srows, 128), F32),
            pltpu.VMEM((ny, 8, 128), F32),
            pltpu.VMEM((2, rows, cols), B16),
            pltpu.VMEM((2, orows, ocols), B16),
            pltpu.SemaphoreType.DMA((2, n)),
            pltpu.SemaphoreType.DMA((2, n)),
            pltpu.SemaphoreType.DMA((2,)),
            pltpu.SemaphoreType.DMA((2,)),
            pltpu.SemaphoreType.DMA((4, n - 1)),
            pltpu.SemaphoreType.DMA((4, n - 1)),
            pltpu.SemaphoreType.DMA((4, many)),
            pltpu.SemaphoreType.DMA((4, many)),
            pltpu.SemaphoreType.DMA((2,)),
            pltpu.SemaphoreType.DMA((2,)),
        ],
        compiler_params=pltpu.CompilerParams(
            collective_id=1, has_side_effects=True, vmem_limit_bytes=48 * 2**20
        ),
        name="reduce_gradients",
    )(pin, pout, psmall, phead)


def passed_along(block, axis, distance):
    devices = range(lax.axis_size(axis))
    route = [(i - distance, i) for i in devices if i - distance in devices]
    return lax.ppermute(block, axis, route)


def silu_slope(value):
    sig = jax.nn.sigmoid(value)
    return sig * (1.0 + value * (1.0 - sig))


def carry_states(decay, local, reverse):
    moved = jnp.zeros_like(local)
    for step in range(lax.axis_size("seq") - 1):
        total = (decay[:, None, None] * moved.astype(F32) + local).astype(B16)
        moved = passed_along(total, "seq", -1 if reverse else 1)
    return moved.astype(F32)


def dot(spec, left, right):
    return jnp.einsum(spec, left, right, preferred_element_type=F32)


def body(
    tokens,
    norm_gain,
    in_weight,
    conv_weight,
    conv_bias,
    dt_bias,
    a_log,
    skip,
    gate_norm,
    out_weight,
    cotangent,
):
    seqs, piece, width = tokens.shape
    n = lax.axis_size("dp")
    ny = lax.axis_size("seq") // 2
    inner = HEADS * HEAD
    chans = inner + 2 * STATE
    rows = in_weight.shape[0]
    orows = out_weight.shape[0]
    edge_rows = KCONV - 1
    spare = chans - inner - HEADS
    half = width // 2
    tokens = tokens[0]
    cotangent = cotangent[0]

    win = jnp.stack(
        [
            in_weight[:, inner : inner + chans],
            jnp.concatenate(
                [
                    in_weight[:, :inner],
                    in_weight[:, inner + chans :],
                    jnp.zeros((rows, spare), B16),
                ],
                1,
            ),
        ]
    )
    wout = jnp.stack([out_weight[:, :half], out_weight[:, half:]])
    parts = (norm_gain, conv_weight.reshape(-1), conv_bias, gate_norm)
    sizes = [part.size for part in parts]
    total = sum(sizes)
    srows = -(-total // 1024) * 8
    small = jnp.pad(jnp.concatenate(parts), (0, srows * 128 - total)).reshape(srows, 128)
    gin, gout, gsmall = gather_all(win, wout, small, n)
    gflat = gsmall.reshape(n, srows * 128)
    cuts = [0]
    for size in sizes:
        cuts.append(cuts[-1] + size)
    norm_full = gflat[:, cuts[0] : cuts[1]].reshape(-1)
    conv_full = jnp.swapaxes(gflat[:, cuts[1] : cuts[2]].reshape(n, KCONV, -1), 0, 1)
    conv_full = conv_full.reshape(KCONV, chans)
    cbias_full = gflat[:, cuts[2] : cuts[3]].reshape(-1)
    gnorm_full = gflat[:, cuts[3] : cuts[4]].reshape(-1)
    w_x = gin[0].reshape(width, chans)
    w_z = gin[1].reshape(width, chans)
    w_o0 = gout[0].reshape(inner, half)
    w_o1 = gout[1].reshape(inner, half)

    x_in = tokens.astype(F32)
    rinv = lax.rsqrt(jnp.mean(x_in * x_in, -1, keepdims=True) + EPS)
    unit = x_in * rinv
    h16 = (unit * norm_full).astype(B16)
    xbc16 = dot("qd,de->qe", h16, w_x).astype(B16)
    zd = dot("qd,de->qe", h16, w_z)
    zval = zd[:, :inner]
    dt_raw = zd[:, inner : inner + HEADS]
    edge = passed_along(xbc16[piece - edge_rows :], "seq", 1)
    padded16 = jnp.concatenate([edge, xbc16], 0)
    pre = cbias_full + conv_full[0] * padded16[0:piece]
    for k in range(1, KCONV):
        pre = pre + conv_full[k] * padded16[k : k + piece]
    xconv = jax.nn.silu(pre)
    xs16 = xconv[:, :inner].astype(B16).reshape(piece, HEADS, HEAD)
    bm16 = xconv[:, inner : inner + STATE].astype(B16)
    cm16 = xconv[:, inner + STATE :].astype(B16)
    shifted = dt_raw + dt_bias
    dth = jax.nn.softplus(shifted).T
    rate = -jnp.exp(a_log)
    lower = jnp.arange(piece)[:, None] >= jnp.arange(piece)[None, :]
    ones = lower.astype(F32)
    highest = lax.Precision.HIGHEST
    cumh = jnp.einsum("hu,tu->ht", dth * rate[:, None], ones, precision=highest)
    seg = jnp.where(lower, cumh[:, :, None] - cumh[:, None, :], -1e30)
    lmat = jnp.exp(seg)
    gram = dot("tn,un->tu", cm16, bm16)
    w16 = (gram[None] * lmat * dth[:, None, :]).astype(B16)
    y_diag = dot("htu,uhp->thp", w16, xs16)
    endc = cumh[:, -1]
    ewt = jnp.exp(endc[:, None] - cumh)
    factor = ewt * dth
    bw16 = (bm16[None] * factor[..., None]).astype(B16)
    s_loc = dot("hun,uhp->hpn", bw16, xs16)
    decay = jnp.exp(endc)
    s_in = carry_states(decay, s_loc, False)
    s_in16 = s_in.astype(B16)
    ecum = jnp.exp(cumh)
    ce16 = (cm16[None] * ecum[..., None]).astype(B16)
    y_off = dot("htn,hpn->thp", ce16, s_in16)
    xsf = xs16.astype(F32)
    yval = (y_diag + y_off + skip[:, None] * xsf).reshape(piece, inner)
    gate_act = jax.nn.silu(zval)
    gated = yval * gate_act
    grinv = lax.rsqrt(jnp.mean(gated * gated, -1, keepdims=True) + EPS)
    gunit = gated * grinv
    n16 = (gunit * gnorm_full).astype(B16)
    branch = jnp.concatenate([dot("qi,id->qd", n16, w_o0), dot("qi,id->qd", n16, w_o1)], -1)
    mixed = (x_in + branch).astype(B16)
    cot0 = cotangent[:, :half]
    cot1 = cotangent[:, half:]
    g_wout = jnp.stack(
        [dot("qi,qd->id", n16, cot0).astype(B16), dot("qi,qd->id", n16, cot1).astype(B16)]
    )
    dnorm = dot("qd,id->qi", cot0, w_o0) + dot("qd,id->qi", cot1, w_o1)
    g_gnorm = jnp.sum(dnorm * gunit, 0)
    dscaled = dnorm * gnorm_full
    dgated = grinv * (dscaled - gunit * jnp.mean(dscaled * gunit, -1, keepdims=True))
    dy16 = (dgated * gate_act).astype(B16).reshape(piece, HEADS, HEAD)
    dz = dgated * yval * silu_slope(zval)
    dyf = dy16.astype(F32)
    g_skip = jnp.sum(dyf * xsf, (0, 2))
    dxs = skip[:, None] * dyf
    dce = dot("thp,hpn->htn", dy16, s_in16)
    ds_loc_in = dot("htn,thp->hpn", ce16, dy16)
    dcm = jnp.sum(dce * ecum[..., None], 0)
    dcum = jnp.sum(dce * cm16[None] * ecum[..., None], -1)
    ds_out = carry_states(decay, ds_loc_in, True)
    dsl16 = ds_out.astype(B16)
    dend = jnp.sum(ds_out * s_in, (1, 2)) * decay
    dbw = dot("hpn,uhp->hun", dsl16, xs16)
    dxs = dxs + dot("hun,hpn->uhp", bw16, dsl16)
    dbm = jnp.sum(dbw * factor[..., None], 0)
    dfactor = jnp.sum(dbw * bm16[None], -1)
    ddt = dfactor * ewt
    dlog = dfactor * factor
    dend = dend + jnp.sum(dlog, -1)
    dcum = dcum - dlog
    dwmat = dot("thp,uhp->htu", dy16, xs16)
    dxs = dxs + dot("htu,thp->uhp", w16, dy16)
    dlmat = dwmat * gram[None] * dth[:, None, :]
    dg16 = jnp.sum(dwmat * lmat * dth[:, None, :], 0).astype(B16)
    ddt = ddt + jnp.sum(dwmat * gram[None] * lmat, 1)
    dseg = dlmat * lmat
    dcum = dcum + jnp.sum(dseg, 2) - jnp.sum(dseg, 1)
    dcm = dcm + dot("tu,un->tn", dg16, bm16)
    dbm = dbm + dot("tu,tn->un", dg16, cm16)
    dcum = dcum + jnp.pad(dend[:, None], ((0, 0), (piece - 1, 0)))
    dda = jnp.einsum("ht,tu->hu", dcum, ones, precision=highest)
    ddt = ddt + dda * rate[:, None]
    g_alog = jnp.sum(dda * dth, 1) * rate
    draw = ddt.T * jax.nn.sigmoid(shifted)
    g_dtb = jnp.sum(draw, 0)
    dxconv = jnp.concatenate([dxs.reshape(piece, inner), dbm, dcm], -1)
    dpre = dxconv * silu_slope(pre)
    g_cbias = jnp.sum(dpre, 0)
    g_conv = jnp.stack([jnp.sum(dpre * padded16[k : k + piece], 0) for k in range(KCONV)])
    dpadded = jnp.pad(conv_full[0] * dpre, ((0, edge_rows), (0, 0)))
    for k in range(1, KCONV):
        dpadded = dpadded + jnp.pad(conv_full[k] * dpre, ((k, edge_rows - k), (0, 0)))
    returned = passed_along(dpadded[:edge_rows], "seq", -1)
    dxbc = dpadded[edge_rows:] + jnp.pad(returned, ((piece - edge_rows, 0), (0, 0)))
    dxbc16 = dxbc.astype(B16)
    dzd16 = jnp.concatenate([dz, draw, jnp.zeros((piece, spare), F32)], -1).astype(B16)
    g_win = jnp.stack(
        [dot("qd,qe->de", h16, dxbc16).astype(B16), dot("qd,qe->de", h16, dzd16).astype(B16)]
    )
    dhid = dot("qe,de->qd", dxbc16, w_x) + dot("qe,de->qd", dzd16, w_z)
    g_norm = jnp.sum(dhid * unit, 0)
    dunit = dhid * norm_full
    dx_in = cotangent.astype(F32) + rinv * (
        dunit - unit * jnp.mean(dunit * unit, -1, keepdims=True)
    )
    grad_tokens = dx_in.astype(B16)

    psmall = jnp.concatenate(
        [
            g_norm.reshape(n, -1),
            jnp.swapaxes(g_conv.reshape(KCONV, n, -1), 0, 1).reshape(n, -1),
            g_cbias.reshape(n, -1),
            g_gnorm.reshape(n, -1),
            jnp.zeros((n, srows * 128 - total), F32),
        ],
        1,
    ).reshape(n, srows, 128)
    phead = jnp.pad(jnp.stack([g_dtb, g_alog, g_skip]), ((0, 5), (0, 128 - HEADS)))
    oin, oout, osmall, ohead = reduce_all(
        g_win.reshape(2, n, rows, chans), g_wout.reshape(2, n, orows, half), psmall, phead, n, ny
    )
    flat = osmall.reshape(-1)
    return (
        mixed[None],
        grad_tokens[None],
        flat[cuts[0] : cuts[1]],
        jnp.concatenate([oin[1, :, :inner], oin[0], oin[1, :, inner : inner + HEADS]], 1),
        flat[cuts[1] : cuts[2]].reshape(KCONV, -1),
        flat[cuts[2] : cuts[3]],
        ohead[0, :HEADS],
        ohead[1, :HEADS],
        ohead[2, :HEADS],
        flat[cuts[3] : cuts[4]],
        jnp.concatenate([oout[0], oout[1]], 1),
    )


def solution(mesh):
    placed = (
        P("dp", "seq", None),
        P("dp"),
        P("dp", None),
        P(None, "dp"),
        P("dp"),
        P(),
        P(),
        P(),
        P("dp"),
        P("dp", None),
        P("dp", "seq", None),
    )
    return jax.shard_map(
        body,
        mesh=mesh,
        in_specs=placed,
        out_specs=(
            P("dp", "seq", None),
            P("dp", "seq", None),
            P("dp"),
            P("dp", None),
            P(None, "dp"),
            P("dp"),
            P(),
            P(),
            P(),
            P("dp"),
            P("dp", None),
        ),
        check_vma=False,
    )
```

```python
import functools

import jax
import jax.numpy as jnp
from jax import lax
from jax.experimental import pallas as pl
from jax.experimental.pallas import tpu as pltpu
from jax.sharding import PartitionSpec as P

HEADS = 24
HEAD = 64
STATE = 128
KCONV = 4
EPS = 1e-05
MESH = pl.DeviceIdType.MESH
F32 = jnp.float32
B16 = jnp.bfloat16


def ring_place(device, n):
    odd = device % 2
    return (1 - odd) * (device // 2) + odd * (n - 1 - device // 2)


def ring_device(place, n):
    place = (place + n) % n
    late = (2 * place) // n
    return (1 - late) * (2 * place) + late * (2 * (n - 1 - place) + 1)


def remote(src, dst, send, recv, target):
    return pltpu.make_async_remote_copy(
        src_ref=src, dst_ref=dst, send_sem=send, recv_sem=recv, device_id=target, device_id_type=MESH
    )


def greet(targets):
    barrier = pltpu.get_barrier_semaphore()
    for target in targets:
        pl.semaphore_signal(barrier, inc=1, device_id=target, device_id_type=MESH)
    pl.semaphore_wait(barrier, len(targets))


def gather_kernel(
    n, win, wout, small, gin, gout, gsmall, ring_send, ring_recv, core_send, core_recv
):
    d = lax.axis_index("dp")
    s = lax.axis_index("seq")
    c = s % 2
    p = ring_place(d, n)
    ahead = (ring_device(p + 1, n), s)
    behind = (ring_device(p - 1, n), s)
    other = (d, s + 1 - 2 * c)
    greet([ahead, behind, other])
    up = n // 2
    down = n - 1 - up
    pending = []

    def hop(index, origin, target, first):
        sources = (
            (win.at[c], wout.at[c], small)
            if first
            else (gin.at[c, origin], gout.at[c, origin], gsmall.at[origin])
        )
        dests = (gin.at[c, origin], gout.at[c, origin], gsmall.at[origin])
        copies = [
            remote(src, dst, ring_send.at[j, index], ring_recv.at[j, index], target)
            for j, (src, dst) in enumerate(zip(sources, dests))
        ]
        for copy in copies:
            copy.start()
        return copies

    def share(index, origin):
        for j, ref in enumerate((gin, gout)):
            copy = remote(
                ref.at[c, origin],
                ref.at[c, origin],
                core_send.at[j, index],
                core_recv.at[j, index],
                other,
            )
            copy.start()
            pending.append(copy)

    cw = hop(0, d, ahead, True)
    ccw = hop(up, d, behind, True)
    gin[0, d] = win[0]
    gin[1, d] = win[1]
    gout[0, d] = wout[0]
    gout[1, d] = wout[1]
    gsmall[d] = small[...]
    sent = list(cw) + list(ccw)
    for k in range(up):
        for copy in cw:
            copy.wait_recv()
        origin = ring_device(p - 1 - k, n)
        if k + 1 < up:
            cw = hop(k + 1, origin, ahead, False)
            sent += cw
        share(k, origin)
        if k < down:
            for copy in ccw:
                copy.wait_recv()
            origin = ring_device(p + 1 + k, n)
            if k + 1 < down:
                ccw = hop(up + k + 1, origin, behind, False)
                sent += ccw
            share(up + k, origin)
    for copy in sent:
        copy.wait_send()
    for copy in pending:
        copy.wait_send()
        copy.wait_recv()


def gather_all(win, wout, small, n):
    _, rows, cols = win.shape
    _, orows, ocols = wout.shape
    srows = small.shape[0]
    vmem = pl.BlockSpec(memory_space=pltpu.VMEM)
    return pl.pallas_call(
        functools.partial(gather_kernel, n),
        out_shape=(
            jax.ShapeDtypeStruct((2, n, rows, cols), B16),
            jax.ShapeDtypeStruct((2, n, orows, ocols), B16),
            jax.ShapeDtypeStruct((n, srows, 128), F32),
        ),
        in_specs=[vmem] * 3,
        out_specs=(vmem,) * 3,
        scratch_shapes=[
            pltpu.SemaphoreType.DMA((3, n - 1)),
            pltpu.SemaphoreType.DMA((3, n - 1)),
            pltpu.SemaphoreType.DMA((2, n - 1)),
            pltpu.SemaphoreType.DMA((2, n - 1)),
        ],
        compiler_params=pltpu.CompilerParams(
            collective_id=0, has_side_effects=True, vmem_limit_bytes=40 * 2**20
        ),
        name="gather_weights",
    )(win, wout, small)


def reduce_kernel(
    n,
    ny,
    pin,
    pout,
    psmall,
    phead,
    oin,
    oout,
    osmall,
    ohead,
    cin,
    cout,
    csmall,
    chead,
    sin,
    sout,
    ssmall,
    rin,
    rout,
    rsmall,
    hall,
    yin,
    yout,
    ysmall,
    yhead,
    fin,
    fout,
    core_send,
    core_recv,
    small_send,
    small_recv,
    ring_send,
    ring_recv,
    y_send,
    y_recv,
    end_send,
    end_recv,
):
    d = lax.axis_index("dp")
    s = lax.axis_index("seq")
    c = s % 2
    y = s // 2
    p = ring_place(d, n)
    ahead = (ring_device(p + 1, n), s)
    behind = (ring_device(p - 1, n), s)
    other = (d, s + 1 - 2 * c)
    peers = [(d, ((y + j) % ny) * 2 + c) for j in range(1, ny)]
    greet([ahead, behind, other] + peers)
    up = n // 2
    down = n - 1 - up
    sent = []

    small_copies = [
        remote(psmall, csmall, small_send.at[0], small_recv.at[0], other),
        remote(phead, chead, small_send.at[1], small_recv.at[1], other),
    ]
    for copy in small_copies:
        copy.start()
    order = []
    for k in range(up):
        order.append(up - k)
        if k < down:
            order.append(k - down)
    order.append(0)
    swaps = {}
    for j, offset in enumerate(order):
        t = ring_device(p + offset, n)
        swaps[offset] = [
            remote(pin.at[1 - c, t], cin.at[t], core_send.at[0, j], core_recv.at[0, j], other),
            remote(pout.at[1 - c, t], cout.at[t], core_send.at[1, j], core_recv.at[1, j], other),
        ]
        for copy in swaps[offset]:
            copy.start()
    for copy in small_copies:
        copy.wait()
    hall[d] = phead[...] + chead[...]

    def partial(offset):
        for copy in swaps[offset]:
            copy.wait_recv()
        t = ring_device(p + offset, n)
        return (
            t,
            pin[c, t].astype(F32) + cin[t].astype(F32),
            pout[c, t].astype(F32) + cout[t].astype(F32),
            psmall[t] + csmall[t],
        )

    def hop(slot, offset, before, origin, target):
        t, a, b, e = partial(offset)
        if before is not None:
            a = a + rin[before].astype(F32)
            b = b + rout[before].astype(F32)
            e = e + rsmall[before]
        sin[t] = a.astype(B16)
        sout[t] = b.astype(B16)
        ssmall[t] = e
        pairs = (
            (sin.at[t], rin.at[slot]),
            (sout.at[t], rout.at[slot]),
            (ssmall.at[t], rsmall.at[slot]),
            (hall.at[origin], hall.at[origin]),
        )
        copies = [
            remote(src, dst, ring_send.at[j, slot], ring_recv.at[j, slot], target)
            for j, (src, dst) in enumerate(pairs)
        ]
        for copy in copies:
            copy.start()
        sent.extend(copies)
        return copies

    cw = None
    ccw = None
    for k in range(up):
        if cw is not None:
            for copy in cw:
                copy.wait_recv()
        cw = hop(k, up - k, k - 1 if k else None, ring_device(p - k, n), ahead)
        if k < down:
            if ccw is not None:
                for copy in ccw:
                    copy.wait_recv()
            slot = up + k
            ccw = hop(slot, k - down, slot - 1 if k else None, ring_device(p + k, n), behind)
    _, a, b, e = partial(0)
    for copy in ccw:
        copy.wait_recv()
    last = up + down - 1
    a = a + rin[last].astype(F32)
    b = b + rout[last].astype(F32)
    e = e + rsmall[last]
    for copy in cw:
        copy.wait_recv()
    a = a + rin[up - 1].astype(F32)
    b = b + rout[up - 1].astype(F32)
    e = e + rsmall[up - 1]
    head = hall[0]
    for j in range(1, n):
        head = head + hall[j]
    yin[y] = a.astype(B16)
    yout[y] = b.astype(B16)
    ysmall[y] = e
    yhead[y] = head
    across = []
    for i, peer in enumerate(peers):
        for j, ref in enumerate((yin, yout, ysmall, yhead)):
            copy = remote(ref.at[y], ref.at[y], y_send.at[j, i], y_recv.at[j, i], peer)
            copy.start()
            across.append(copy)
    for copy in across:
        copy.wait_recv()
    a = yin[0].astype(F32)
    b = yout[0].astype(F32)
    e = ysmall[0]
    head = yhead[0]
    for j in range(1, ny):
        a = a + yin[j].astype(F32)
        b = b + yout[j].astype(F32)
        e = e + ysmall[j]
        head = head + yhead[j]
    fin[c] = a.astype(B16)
    fout[c] = b.astype(B16)
    ends = [
        remote(fin.at[c], fin.at[c], end_send.at[0], end_recv.at[0], other),
        remote(fout.at[c], fout.at[c], end_send.at[1], end_recv.at[1], other),
    ]
    for copy in ends:
        copy.start()
    osmall[...] = e
    ohead[...] = head
    for offset in order:
        for copy in swaps[offset]:
            copy.wait_send()
    for copy in sent:
        copy.wait_send()
    for copy in across:
        copy.wait_send()
    for copy in ends:
        copy.wait()
    oin[...] = fin[...].astype(F32)
    oout[...] = fout[...].astype(F32)


def reduce_all(pin, pout, psmall, phead, n, ny):
    _, _, rows, cols = pin.shape
    _, _, orows, ocols = pout.shape
    srows = psmall.shape[1]
    vmem = pl.BlockSpec(memory_space=pltpu.VMEM)
    many = max(ny - 1, 1)
    return pl.pallas_call(
        functools.partial(reduce_kernel, n, ny),
        out_shape=(
            jax.ShapeDtypeStruct((2, rows, cols), F32),
            jax.ShapeDtypeStruct((2, orows, ocols), F32),
            jax.ShapeDtypeStruct((srows, 128), F32),
            jax.ShapeDtypeStruct((8, 128), F32),
        ),
        in_specs=[vmem] * 4,
        out_specs=(vmem,) * 4,
        scratch_shapes=[
            pltpu.VMEM((n, rows, cols), B16),
            pltpu.VMEM((n, orows, ocols), B16),
            pltpu.VMEM((n, srows, 128), F32),
            pltpu.VMEM((8, 128), F32),
            pltpu.VMEM((n, rows, cols), B16),
            pltpu.VMEM((n, orows, ocols), B16),
            pltpu.VMEM((n, srows, 128), F32),
            pltpu.VMEM((n - 1, rows, cols), B16),
            pltpu.VMEM((n - 1, orows, ocols), B16),
            pltpu.VMEM((n - 1, srows, 128), F32),
            pltpu.VMEM((n, 8, 128), F32),
            pltpu.VMEM((ny, rows, cols), B16),
            pltpu.VMEM((ny, orows, ocols), B16),
            pltpu.VMEM((ny, srows, 128), F32),
            pltpu.VMEM((ny, 8, 128), F32),
            pltpu.VMEM((2, rows, cols), B16),
            pltpu.VMEM((2, orows, ocols), B16),
            pltpu.SemaphoreType.DMA((2, n)),
            pltpu.SemaphoreType.DMA((2, n)),
            pltpu.SemaphoreType.DMA((2,)),
            pltpu.SemaphoreType.DMA((2,)),
            pltpu.SemaphoreType.DMA((4, n - 1)),
            pltpu.SemaphoreType.DMA((4, n - 1)),
            pltpu.SemaphoreType.DMA((4, many)),
            pltpu.SemaphoreType.DMA((4, many)),
            pltpu.SemaphoreType.DMA((2,)),
            pltpu.SemaphoreType.DMA((2,)),
        ],
        compiler_params=pltpu.CompilerParams(
            collective_id=1, has_side_effects=True, vmem_limit_bytes=48 * 2**20
        ),
        name="reduce_gradients",
    )(pin, pout, psmall, phead)


def passed_along(block, axis, distance):
    devices = range(lax.axis_size(axis))
    route = [(i - distance, i) for i in devices if i - distance in devices]
    return lax.ppermute(block, axis, route)


def silu_slope(value):
    sig = jax.nn.sigmoid(value)
    return sig * (1.0 + value * (1.0 - sig))


def carry_states(decay, local, reverse):
    moved = jnp.zeros_like(local, dtype=B16)
    for step in range(lax.axis_size("seq") - 1):
        total = (decay * moved.astype(F32) + local).astype(B16)
        moved = passed_along(total, "seq", -1 if reverse else 1)
    return moved


def mm(left, right, dims=((1,), (0,)), precision=None):
    return lax.dot_general(
        left, right, (dims, ((), ())), precision=precision, preferred_element_type=F32
    )


NT = ((1,), (1,))
TN = ((0,), (0,))
HIGHEST = lax.Precision.HIGHEST


def head_map():
    lane = lax.broadcasted_iota(jnp.int32, (128, HEADS * HEAD), 1) // HEAD
    return (lane == lax.broadcasted_iota(jnp.int32, (128, HEADS * HEAD), 0)).astype(B16)


def split(value):
    high = value.astype(B16)
    return high, (value - high.astype(F32)).astype(B16)


def spread(value):
    high, rest = split(value)
    place = head_map()
    return mm(high, place) + mm(rest, place)


def gathered(value):
    high, rest = split(value)
    place = head_map()
    return mm(high, place, NT) + mm(rest, place, NT)


def triangle(piece):
    row = lax.broadcasted_iota(jnp.int32, (piece, piece), 0)
    return row >= lax.broadcasted_iota(jnp.int32, (piece, piece), 1)


def pair_masks(shape):
    first = lax.broadcasted_iota(jnp.int32, shape, 1) < HEAD
    return first, jnp.logical_not(first)


def local_call(kernel, outs, *args):
    vmem = pl.BlockSpec(memory_space=pltpu.VMEM)
    shapes = tuple(jax.ShapeDtypeStruct(shape, dtype) for shape, dtype in outs)
    moved = sum(a.size * a.dtype.itemsize for a in args)
    return pl.pallas_call(
        kernel,
        out_shape=shapes,
        in_specs=[vmem] * len(args),
        out_specs=(vmem,) * len(outs),
        compiler_params=pltpu.CompilerParams(vmem_limit_bytes=44 * 2**20),
        cost_estimate=pl.CostEstimate(
            flops=10**9 * 5, bytes_accessed=moved, transcendentals=10**6
        ),
        name=kernel.__name__,
    )(*args)


def project(tok, norm, gin, conv, cbias, dtb, rate, h, xbc, pre, z, shift, dt, cum, xs, bm, cm, sloc, decay):
    piece = h.shape[0]
    inner = HEADS * HEAD
    x = tok[...].astype(F32)
    rinv = lax.rsqrt(jnp.mean(x * x, -1, keepdims=True) + EPS)
    h16 = (x * rinv * norm[...]).astype(B16)
    h[...] = h16[8:]
    padded16 = mm(h16, gin[0]).astype(B16)
    xbc[...] = padded16
    padded = padded16.astype(F32)
    zd = mm(h16[8:], gin[1])
    z[...] = zd[:, :inner]
    p = cbias[...] + conv[0:1] * padded[5 : 5 + piece]
    for k in range(1, KCONV):
        p = p + conv[k : k + 1] * padded[5 + k : 5 + k + piece]
    pre[...] = p
    xconv = (p * jax.nn.sigmoid(p)).astype(B16)
    xs16 = xconv[:, :inner]
    b16 = xconv[:, inner : inner + STATE]
    xs[...] = xs16
    bm[...] = b16
    cm[...] = xconv[:, inner + STATE :]
    shifted = zd[:, inner : inner + 128] + dtb[...]
    shift[...] = shifted
    step = jnp.maximum(shifted, 0.0) + jnp.log1p(jnp.exp(-jnp.abs(shifted)))
    dt[...] = step
    total = mm(triangle(piece).astype(F32), step * rate[...], precision=HIGHEST)
    cum[...] = total
    endc = total[piece - 1 : piece]
    xf = (xs16.astype(F32) * spread(jnp.exp(endc - total) * step)).astype(B16)
    sloc[...] = mm(b16, xf, TN)
    decay[...] = spread(jnp.broadcast_to(jnp.exp(endc), (8, 128)))


def diagonal(xs, bm, cm, dt, cum, y):
    piece = xs.shape[0]
    gram = mm(cm[...], bm[...], NT)
    lower = triangle(piece)
    cumc = cum[...]
    cumr = cumc.T
    dtr = dt[...].T
    masks = pair_masks((piece, 128))
    zero = jnp.zeros((piece, 128), B16)
    for j in range(HEADS // 2):
        pair = xs[:, 128 * j : 128 * j + 128]
        out = None
        for i in range(2):
            k = 2 * j + i
            seg = jnp.where(lower, cumc[:, k : k + 1] - cumr[k : k + 1], -1e30)
            w = (gram * jnp.exp(seg) * dtr[k : k + 1]).astype(B16)
            part = mm(w, jnp.where(masks[i], pair, zero))
            out = part if out is None else out + part
        y[:, 128 * j : 128 * j + 128] = out


def gate(tok, sin, ydiag, xs, cm, cum, z, skip, gnorm, gout, cot, mixed, normed, dy, dz, ggn, gsk, dsl, dcm, dcum):
    half = tok.shape[1] // 2
    ecx = spread(jnp.exp(cum[...]))
    s16 = sin[...]
    yoff = mm(cm[...], s16) * ecx
    xsf = xs[...].astype(F32)
    y = ydiag[...] + yoff + skip[...] * xsf
    zv = z[...]
    sig = jax.nn.sigmoid(zv)
    act = zv * sig
    gated = y * act
    grinv = lax.rsqrt(jnp.mean(gated * gated, -1, keepdims=True) + EPS)
    gunit = gated * grinv
    n16 = (gunit * gnorm[...]).astype(B16)
    normed[...] = n16
    for i in range(2):
        cols = slice(half * i, half * i + half)
        mixed[:, cols] = (tok[:, cols].astype(F32) + mm(n16, gout[i])).astype(B16)
    dn = mm(cot[:, :half], gout[0], NT) + mm(cot[:, half:], gout[1], NT)
    ggn[...] = jnp.sum(dn * gunit, 0, keepdims=True)
    ds = dn * gnorm[...]
    dgated = grinv * (ds - gunit * jnp.mean(ds * gunit, -1, keepdims=True))
    dy16 = (dgated * act).astype(B16)
    dy[...] = dy16
    dz[...] = (dgated * y * (sig * (1.0 + zv * (1.0 - sig)))).astype(B16)
    dyf = dy16.astype(F32)
    gsk[...] = jnp.sum(dyf * xsf, 0, keepdims=True)
    dye = (dyf * ecx).astype(B16)
    dsl[...] = mm(cm[...], dye, TN)
    dcm[...] = mm(dye, s16, NT)
    dcum[...] = gathered(dyf * yoff)


def diagonal_back(xs, bm, cm, dt, cum, dy, normed, cot, dxs, ddt, dcum, dcm, dbm, gw, rows):
    piece = xs.shape[0]
    half = cot.shape[1] // 2
    gw[0] = mm(normed[...], cot[:, :half], TN).astype(B16)
    gw[1] = mm(normed[...], cot[:, half:], TN).astype(B16)
    gram = mm(cm[...], bm[...], NT)
    lower = triangle(piece)
    cumc = cum[...]
    cumr = cumc.T
    dtr = dt[...].T
    masks = pair_masks((piece, 128))
    zero = jnp.zeros((piece, 128), B16)
    lane = lax.broadcasted_iota(jnp.int32, (piece, 128), 1)
    dcum[...] = jnp.zeros((piece, 128), F32)
    rows[...] = jnp.zeros((128, piece), F32)
    dg = jnp.zeros((piece, piece), F32)
    for j in range(HEADS // 2):
        cols = slice(128 * j, 128 * j + 128)
        pair = xs[:, cols]
        dpair = dy[:, cols]
        out = None
        for i in range(2):
            k = 2 * j + i
            seg = jnp.where(lower, cumc[:, k : k + 1] - cumr[k : k + 1], -1e30)
            lmat = jnp.exp(seg)
            dmask = jnp.where(masks[i], dpair, zero)
            dw = mm(dmask, pair, NT)
            row = dtr[k : k + 1]
            w = (gram * lmat * row).astype(B16)
            part = mm(w, dmask, TN)
            out = part if out is None else out + part
            q = dw * lmat
            dg = dg + q * row
            gl = q * gram
            rows[k : k + 1, :] = jnp.sum(gl, 0, keepdims=True)
            col = jnp.sum(gl * row, 1, keepdims=True)
            dcum[...] = jnp.where(lane == k, col, dcum[...])
        dxs[:, cols] = out
    ddt[...] = rows[...].T
    dcum[...] = dcum[...] - ddt[...] * dt[...]
    dg16 = dg.astype(B16)
    dcm[...] = mm(dg16, bm[...])
    dbm[...] = mm(dg16, cm[...], TN)


def state_back(dso, sin, decay, xs, bm, dt, cum, dy, dxsd, ddtq, dcumq, dcmq, dbmq, dcum3, dcm3, skip, pre, xbc, shift, rate, dpre, draw, gdtb, galog, gcb, gconv):
    piece = xs.shape[0]
    inner = HEADS * HEAD
    d16 = dso[...]
    cumc = cum[...]
    ewt = jnp.exp(cumc[piece - 1 : piece] - cumc)
    step = dt[...]
    factor = ewt * step
    facx = spread(factor)
    xsf = xs[...].astype(F32)
    t = mm(bm[...], d16)
    dxs = skip[...] * dy[...].astype(F32) + facx * t + dxsd[...]
    dfactor = gathered(xsf * t)
    dbm = mm((xsf * facx).astype(B16), d16, NT) + dbmq[...]
    dcm = dcm3[...] + dcmq[...]
    dlog = dfactor * factor
    states = jnp.sum(d16.astype(F32) * sin[...].astype(F32), 0, keepdims=True) * decay[0:1]
    dend = gathered(jnp.broadcast_to(states, (8, inner)))[0:1]
    dend = dend + jnp.sum(dlog, 0, keepdims=True)
    dcum = dcum3[...] + dcumq[...] - dlog
    last = lax.broadcasted_iota(jnp.int32, (piece, 128), 0) == piece - 1
    dcum = dcum + jnp.where(last, dend, 0.0)
    dda = mm(triangle(piece).astype(F32), dcum, TN, HIGHEST)
    ddt = dfactor * ewt + ddtq[...] + dda * rate[...]
    galog[...] = jnp.sum(dda * step, 0, keepdims=True) * rate[...]
    dr = ddt * jax.nn.sigmoid(shift[...])
    gdtb[...] = jnp.sum(dr, 0, keepdims=True)
    draw[...] = dr.astype(B16)
    padded = xbc[...].astype(F32)
    for lo, hi, val in (
        (0, inner, dxs),
        (inner, inner + STATE, dbm),
        (inner + STATE, inner + 2 * STATE, dcm),
    ):
        dp = val * silu_slope(pre[:, lo:hi])
        dpre[:, lo:hi] = dp
        gcb[:, lo:hi] = jnp.sum(dp, 0, keepdims=True)
        for k in range(KCONV):
            gconv[k : k + 1, lo:hi] = jnp.sum(
                dp * padded[5 + k : 5 + k + piece, lo:hi], 0, keepdims=True
            )


def finish(dpre, after, conv, h, dz, draw, gin, tok, cot, norm, gw, gtok, gnorm):
    piece = dpre.shape[0]
    ext = jnp.concatenate([dpre[...], after[...]], 0)
    dx = conv[KCONV - 1 : KCONV] * ext[:piece]
    for k in range(KCONV - 1):
        shift = KCONV - 1 - k
        dx = dx + conv[k : k + 1] * ext[shift : shift + piece]
    dx16 = dx.astype(B16)
    inner = dz.shape[1]
    spare = dpre.shape[1] - inner - 128
    dzd = jnp.concatenate([dz[...], draw[...], jnp.zeros((piece, spare), B16)], 1)
    gw[0] = mm(h[...], dx16, TN).astype(B16)
    gw[1] = mm(h[...], dzd, TN).astype(B16)
    dh = mm(dx16, gin[0], NT) + mm(dzd, gin[1], NT)
    x = tok[...].astype(F32)
    rinv = lax.rsqrt(jnp.mean(x * x, -1, keepdims=True) + EPS)
    unit = x * rinv
    gnorm[...] = jnp.sum(dh * unit, 0, keepdims=True)
    du = dh * norm[...]
    gtok[...] = (
        cot[...].astype(F32) + rinv * (du - unit * jnp.mean(du * unit, -1, keepdims=True))
    ).astype(B16)


def body(
    tokens,
    norm_gain,
    in_weight,
    conv_weight,
    conv_bias,
    dt_bias,
    a_log,
    skip,
    gate_norm,
    out_weight,
    cotangent,
):
    seqs, piece, width = tokens.shape
    n = lax.axis_size("dp")
    ny = lax.axis_size("seq") // 2
    inner = HEADS * HEAD
    chans = inner + 2 * STATE
    rows = in_weight.shape[0]
    orows = out_weight.shape[0]
    edge_rows = 8
    spare = chans - inner - HEADS
    half = width // 2
    tokens = tokens[0]
    cotangent = cotangent[0]

    before = passed_along(tokens[piece - edge_rows :], "seq", 1)
    win = jnp.stack(
        [
            in_weight[:, inner : inner + chans],
            jnp.concatenate(
                [
                    in_weight[:, :inner],
                    in_weight[:, inner + chans :],
                    jnp.zeros((rows, spare), B16),
                ],
                1,
            ),
        ]
    )
    wout = jnp.stack([out_weight[:, :half], out_weight[:, half:]])
    parts = (norm_gain, conv_weight.reshape(-1), conv_bias, gate_norm)
    sizes = [part.size for part in parts]
    total = sum(sizes)
    srows = -(-total // 1024) * 8
    small = jnp.pad(jnp.concatenate(parts), (0, srows * 128 - total)).reshape(srows, 128)
    gin, gout, gsmall = gather_all(win, wout, small, n)
    gflat = gsmall.reshape(n, srows * 128)
    cuts = [0]
    for size in sizes:
        cuts.append(cuts[-1] + size)
    norm_full = gflat[:, cuts[0] : cuts[1]].reshape(-1)
    conv_full = jnp.swapaxes(gflat[:, cuts[1] : cuts[2]].reshape(n, KCONV, -1), 0, 1)
    conv_full = conv_full.reshape(KCONV, chans)
    cbias_full = gflat[:, cuts[2] : cuts[3]].reshape(-1)
    gnorm_full = gflat[:, cuts[3] : cuts[4]].reshape(-1)
    gin = gin.reshape(2, width, chans)
    gout = gout.reshape(2, inner, half)
    norm_full = norm_full[None]
    cbias_full = cbias_full[None]
    gnorm_full = gnorm_full[None]
    lanes = ((0, 0), (0, 128 - HEADS))
    dtb = jnp.pad(dt_bias[None], lanes)
    rate = jnp.pad(-jnp.exp(a_log)[None], lanes)
    skipx = jnp.repeat(skip, HEAD)[None]
    tok_ext = jnp.concatenate([before, tokens], 0)
    heads = ((piece, 128), F32)
    wide = ((piece, inner), F32)
    wide16 = ((piece, inner), B16)
    thin16 = ((piece, STATE), B16)
    thin = ((piece, STATE), F32)
    state = ((STATE, inner), F32)
    h16, xbc, pre, z, shift, dt, cum, xs, bm, cm, s_loc, decay = local_call(
        project,
        (
            ((piece, width), B16),
            ((piece + edge_rows, chans), B16),
            ((piece, chans), F32),
            wide,
            heads,
            heads,
            heads,
            wide16,
            thin16,
            thin16,
            state,
            ((8, inner), F32),
        ),
        *(tok_ext, norm_full, gin, conv_full, cbias_full, dtb, rate),
    )
    (ydiag,) = local_call(diagonal, (wide,), xs, bm, cm, dt, cum)
    s_in = carry_states(decay[0:1], s_loc, False)
    mixed, n16, dy, dz, g_gnorm, g_skip, dsl, dcm3, dcum3 = local_call(
        gate,
        (
            ((piece, width), B16),
            wide16,
            wide16,
            wide16,
            ((1, inner), F32),
            ((1, inner), F32),
            state,
            thin,
            heads,
        ),
        *(tokens, s_in, ydiag, xs, cm, cum, z, skipx, gnorm_full, gout, cotangent),
    )
    dxsd, ddtq, dcumq, dcmq, dbmq, g_wout, _ = local_call(
        diagonal_back,
        (wide, heads, heads, thin, thin, ((2, inner, half), B16), ((128, piece), F32)),
        *(xs, bm, cm, dt, cum, dy, n16, cotangent),
    )
    ds_out = carry_states(decay[0:1], dsl, True)
    dpre, draw, g_dtb, g_alog, g_cbias, g_conv = local_call(
        state_back,
        (
            ((piece, chans), F32),
            ((piece, 128), B16),
            ((1, 128), F32),
            ((1, 128), F32),
            ((1, chans), F32),
            ((KCONV, chans), F32),
        ),
        *(ds_out, s_in, decay, xs, bm, dt, cum, dy, dxsd, ddtq, dcumq, dcmq, dbmq, dcum3, dcm3),
        *(skipx, pre, xbc, shift, rate),
    )
    after = passed_along(dpre[:edge_rows], "seq", -1)
    g_win, grad_tokens, g_norm = local_call(
        finish,
        (((2, width, chans), B16), ((piece, width), B16), ((1, width), F32)),
        *(dpre, after, conv_full, h16, dz, draw, gin, tokens, cotangent, norm_full),
    )
    g_skip = jnp.sum(g_skip.reshape(HEADS, HEAD), 1)

    psmall = jnp.concatenate(
        [
            g_norm.reshape(n, -1),
            jnp.swapaxes(g_conv.reshape(KCONV, n, -1), 0, 1).reshape(n, -1),
            g_cbias.reshape(n, -1),
            g_gnorm.reshape(n, -1),
            jnp.zeros((n, srows * 128 - total), F32),
        ],
        1,
    ).reshape(n, srows, 128)
    phead = jnp.pad(
        jnp.concatenate([g_dtb, g_alog, jnp.pad(g_skip[None], lanes)], 0), ((0, 5), (0, 0))
    )
    oin, oout, osmall, ohead = reduce_all(
        g_win.reshape(2, n, rows, chans), g_wout.reshape(2, n, orows, half), psmall, phead, n, ny
    )
    flat = osmall.reshape(-1)
    return (
        mixed[None],
        grad_tokens[None],
        flat[cuts[0] : cuts[1]],
        jnp.concatenate([oin[1, :, :inner], oin[0], oin[1, :, inner : inner + HEADS]], 1),
        flat[cuts[1] : cuts[2]].reshape(KCONV, -1),
        flat[cuts[2] : cuts[3]],
        ohead[0, :HEADS],
        ohead[1, :HEADS],
        ohead[2, :HEADS],
        flat[cuts[3] : cuts[4]],
        jnp.concatenate([oout[0], oout[1]], 1),
    )


def solution(mesh):
    placed = (
        P("dp", "seq", None),
        P("dp"),
        P("dp", None),
        P(None, "dp"),
        P("dp"),
        P(),
        P(),
        P(),
        P("dp"),
        P("dp", None),
        P("dp", "seq", None),
    )
    return jax.shard_map(
        body,
        mesh=mesh,
        in_specs=placed,
        out_specs=(
            P("dp", "seq", None),
            P("dp", "seq", None),
            P("dp"),
            P("dp", None),
            P(None, "dp"),
            P("dp"),
            P(),
            P(),
            P(),
            P("dp"),
            P("dp", None),
        ),
        check_vma=False,
    )
```
